32 devices in a mesh: grp: 4 (over y, core), blk: 8 (over z, x).
Axes of the slice: x: 2, y: 2, z: 4, core: 2. Of those that a mesh axis runs over, the one named last changes fastest.
Arguments:
- grads: bfloat16 [32, 256, 128], P(('grp', 'blk')), may hold values from -6 to 6
- picks: int32 [32, 256], P(('grp', 'blk')), may hold values from 0 to 511, as said below
- slot_map: int32 [32, 512], P(('grp', 'blk')), may hold values from 0 to 511, each once within a row
- momentum: float32 [16384, 128], P(('grp', 'blk')), may hold values from -6 to 6
- params: float32 [16384, 128], P(('grp', 'blk')), may hold values from -6 to 6
Outputs:
- new_momentum: float32 [16384, 128], P(('grp', 'blk'))
- new_params: float32 [16384, 128], P(('grp', 'blk'))
The draws below stay inside these ranges and needn't reach their ends.
Inputs may be any that keep to these rules, and one draw needn't show every extreme that they name: `picks`: for each replica and owner, the 8 entries in order: the j-th lies in [j * 64, (j + 1) * 64). `slot_map`: each row is a permutation of the 512 slots.
All inputs are finite; a program needn't handle non-finite values.
Results may differ from the reference program's by a relative error of at most 0.0003.
Values may be sent and summed in bfloat16 or wider, within the bound.
A program may use at most 64 MiB of HBM per device.

```python
import jax
import jax.numpy as jnp
from jax import lax

BLOCK = 128
PICK = 8
OWN = 512
ITEMS = 256
TOTAL = 16384
DEVICES = 32


def draw_picks(key, part):
    width = OWN // PICK
    offsets = jax.random.randint(key, (DEVICES, DEVICES, PICK), 0, width, dtype=jnp.int32)
    starts = jnp.arange(PICK, dtype=jnp.int32) * width
    return (offsets + starts[None, None, :]).reshape(DEVICES, DEVICES * PICK)


def steps_of(stream_key, shape, shards, low, top_value):
    def one(axis_at, shards_of):
        heights = jax.random.uniform(jax.random.fold_in(jax.random.fold_in(stream_key, 6), axis_at), (shards_of,), jnp.float32, low / len(shards), top_value / len(shards))
        return jnp.repeat(jnp.exp(heights), shape[axis_at] // shards_of).reshape((-1,) + (1,) * (len(shape) - axis_at - 1))

    gain = one(*shards[0])
    for cut in shards[1:]:
        gain = gain * one(*cut)
    return gain


def bell_draw(stream_key, shape, spread, bound, shards=(), kind=jnp.bfloat16):
    gain = steps_of(stream_key, shape, shards, -0.22, 0.18) if shards else 1.0
    values = jax.random.normal(stream_key, shape, jnp.float32) * spread * gain
    return jnp.minimum(jnp.maximum(values, -bound), bound).astype(kind)


def setup_inputs(seed: int = 0) -> dict:
    arg_keys = jax.random.split(jax.random.key(seed), 6)
    return {
        "grads": bell_draw(arg_keys[0], (DEVICES, ITEMS, BLOCK), 1.0, 6.0, ((0, 32),)),
        "picks": draw_picks(jax.random.fold_in(arg_keys[5], 71), 0),
        "slot_map": jax.vmap(lambda own: jax.random.permutation(own, OWN))(jax.random.split(arg_keys[2], DEVICES)).reshape((DEVICES, OWN)).astype(jnp.int32),
        "momentum": bell_draw(arg_keys[3], (TOTAL, BLOCK), 1.0, 6.0, ((0, 32),), jnp.float32),
        "params": bell_draw(arg_keys[4], (TOTAL, BLOCK), 1.0, 6.0, ((0, 32),), jnp.float32),
    }


def reference(grads, picks, slot_map, momentum, params):
    owners = slot_map.shape[0]
    owned = slot_map.shape[1]
    block = grads.shape[-1]
    owner_item = jnp.repeat(jnp.arange(owners, dtype=jnp.int32), PICK)

    def add_replica(total, inputs):
        values, chosen = inputs
        slots = slot_map[owner_item, chosen].astype(jnp.int32) + owner_item * owned
        return total.at[slots].add(values.astype(jnp.float32)), None

    start = jnp.zeros((owners * owned, block), jnp.float32)
    gradient, _ = lax.scan(add_replica, start, (grads, picks))
    new_momentum = 0.9 * momentum + gradient
    new_params = params - 0.05 * (gradient + 0.9 * new_momentum)
    return new_momentum, new_params
```

```python
import functools

import jax
import jax.numpy as jnp
from jax import lax
from jax.experimental import pallas as pl
from jax.experimental.pallas import tpu as pltpu
from jax.sharding import PartitionSpec as P

MESH = pl.DeviceIdType.MESH


def exchange(groups, columns, grads_hbm, picks_hbm, slots_hbm, out_ref, grads, picks, slots,
             send, recv, load_sem, send_sem, recv_sem):
    peers = groups * columns
    items, block = grads.shape
    owned = slots.shape[1]
    count = items // peers
    width = owned // count
    per_tile = block // width
    tiles = owned // block
    g = lax.axis_index("grp")
    b = lax.axis_index("blk")
    me = g * columns + b

    loads = [
        pltpu.make_async_copy(picks_hbm, picks, load_sem.at[0]),
        pltpu.make_async_copy(grads_hbm, grads, load_sem.at[1]),
        pltpu.make_async_copy(slots_hbm, slots, load_sem.at[2]),
    ]
    for load in loads:
        load.start()

    def place(k):
        other = lax.rem(me + k, peers)
        return other, (other // columns, lax.rem(other, columns))

    def each_peer(act):
        if peers <= 64:
            for k in range(1, peers):
                act(k)
        else:
            lax.fori_loop(1, peers, lambda k, c: (act(k), c)[1], 0)

    barrier = pltpu.get_barrier_semaphore()

    def greet(k):
        pl.semaphore_signal(barrier, inc=1, device_id=place(k)[1], device_id_type=MESH)

    each_peer(greet)

    loads[0].wait()
    numbers = jnp.broadcast_to(picks[...].astype(jnp.float32), (block, items)).T
    row = lax.broadcasted_iota(jnp.int32, (items, block), 0) % count
    lane = lax.broadcasted_iota(jnp.int32, (items, block), 1)
    base = (row // per_tile) * block
    hot = (numbers == (lane + base).astype(jnp.float32)).astype(jnp.float32)
    loads[1].wait()
    values = grads[...].astype(jnp.float32)
    packed = jnp.concatenate(
        [values.reshape(peers, count, block), hot.reshape(peers, count, block)], axis=1
    ).astype(jnp.bfloat16)
    send[...] = packed

    pl.semaphore_wait(barrier, peers - 1)

    def ship(k):
        other, where = place(k)
        pltpu.make_async_remote_copy(
            src_ref=send.at[other],
            dst_ref=recv.at[me],
            send_sem=send_sem,
            recv_sem=recv_sem,
            device_id=where,
            device_id_type=MESH,
        ).start()

    each_peer(ship)
    recv[me] = send[me]

    loads[2].wait()
    table = slots[...].astype(jnp.float32)
    high = jnp.floor(table * (1.0 / 256.0))
    low = table - 256.0 * high
    rows = [part[:, t * block : (t + 1) * block] for part in (low, high) for t in range(tiles)]
    rows += [jnp.zeros((1, block), jnp.float32)] * (-len(rows) % 16)
    lookup = jnp.concatenate(rows, axis=0).astype(jnp.bfloat16)

    done = pltpu.make_async_remote_copy(
        src_ref=send.at[pl.ds(0, peers - 1)],
        dst_ref=recv.at[pl.ds(0, peers - 1)],
        send_sem=send_sem,
        recv_sem=recv_sem,
        device_id=place(1)[1],
        device_id_type=MESH,
    )
    done.wait_recv()

    group = min(peers, 256 // count)
    chunk = group * count

    def part(i):
        got = recv[pl.ds(i * group, group)].astype(jnp.float32)
        vals = got[:, :count].reshape(chunk, block).astype(jnp.bfloat16)
        ones = got[:, count:].reshape(chunk, block).astype(jnp.bfloat16)
        found = lax.dot_general(
            lookup, ones, (((1,), (1,)), ((), ())), preferred_element_type=jnp.float32
        )
        where = lax.broadcasted_iota(jnp.int32, (1, chunk), 1) % count // per_tile
        slot = jnp.zeros((1, chunk), jnp.float32)
        for t in range(tiles):
            slot = jnp.where(
                where == t, found[t : t + 1] + 256.0 * found[tiles + t : tiles + t + 1], slot
            )
        number = lax.broadcasted_iota(jnp.int32, (owned, chunk), 0).astype(jnp.float32)
        put = (number == slot).astype(jnp.float32).astype(jnp.bfloat16)
        return jnp.dot(put, vals, preferred_element_type=jnp.float32)

    if peers == group:
        out_ref[...] = part(0)
    else:
        out_ref[...] = jnp.zeros_like(out_ref)

        def step(i, c):
            out_ref[...] += part(i)
            return c

        lax.fori_loop(0, peers // group, step, 0)
    done.wait_send()


def shards(grads, picks, slot_map, momentum, params):
    groups = lax.axis_size("grp")
    columns = lax.axis_size("blk")
    peers = groups * columns
    items, block = grads.shape[1:]
    owned = slot_map.shape[1]
    count = items // peers
    gradient = pl.pallas_call(
        functools.partial(exchange, groups, columns),
        out_shape=jax.ShapeDtypeStruct((owned, block), jnp.float32),
        in_specs=[pl.BlockSpec(memory_space=pl.ANY)] * 3,
        out_specs=pl.BlockSpec(memory_space=pltpu.VMEM),
        scratch_shapes=[
            pltpu.VMEM((items, block), jnp.bfloat16),
            pltpu.VMEM((1, items), jnp.int32),
            pltpu.VMEM((1, owned), jnp.int32),
            pltpu.VMEM((peers, 2 * count, block), jnp.bfloat16),
            pltpu.VMEM((peers, 2 * count, block), jnp.bfloat16),
            pltpu.SemaphoreType.DMA((3,)),
            pltpu.SemaphoreType.DMA,
            pltpu.SemaphoreType.DMA,
        ],
        compiler_params=pltpu.CompilerParams(
            collective_id=0, has_side_effects=True, vmem_limit_bytes=40 * 1024 * 1024
        ),
    )(grads[0], picks, slot_map)
    new_momentum = 0.9 * momentum + gradient
    new_params = params - 0.05 * (gradient + 0.9 * new_momentum)
    return (new_momentum, new_params)


def solution(mesh):
    placed = (
        P(("grp", "blk"), None, None),
        P(("grp", "blk"), None),
        P(("grp", "blk"), None),
        P(("grp", "blk"), None),
        P(("grp", "blk"), None),
    )
    return jax.shard_map(
        shards,
        mesh=mesh,
        in_specs=placed,
        out_specs=(P(("grp", "blk"), None), P(("grp", "blk"), None)),
        check_vma=False,
    )
```

```python
import functools

import jax
import jax.numpy as jnp
from jax import lax
from jax.experimental import pallas as pl
from jax.experimental.pallas import tpu as pltpu
from jax.sharding import PartitionSpec as P

MESH = pl.DeviceIdType.MESH


def powers(*sizes):
    return all(size & (size - 1) == 0 for size in sizes)


def exchange(groups, columns, grads_hbm, picks_hbm, slots_hbm, momentum_hbm, params_hbm,
             recv, lookup, momentum, params, grads, picks, slots, send,
             load_sem, send_sem, recv_sem):
    peers = groups * columns
    items, block = grads.shape
    owned = slots.shape[1]
    count = items // peers
    width = owned // count
    per_tile = block // width
    tiles = owned // block
    g = lax.axis_index("grp")
    b = lax.axis_index("blk")
    me = g * columns + b

    loads = [
        pltpu.make_async_copy(source, target, load_sem.at[i])
        for i, (source, target) in enumerate(
            [
                (picks_hbm, picks),
                (grads_hbm, grads),
                (slots_hbm, slots),
                (momentum_hbm, momentum),
                (params_hbm, params),
            ]
        )
    ]
    for load in loads[:3]:
        load.start()

    def place(dg, db):
        if powers(groups, columns):
            return g ^ dg, b ^ db
        return lax.rem(g + dg, groups), lax.rem(b + db, columns)

    def each_peer(act):
        if peers <= 64:
            for db in reversed(range(columns)):
                for dg in reversed(range(groups)):
                    if dg or db:
                        act(*place(dg, db))
        else:
            def step(k, c):
                act(*place(k // columns, lax.rem(k, columns)))
                return c

            lax.fori_loop(1, peers, step, 0)

    barrier = pltpu.get_barrier_semaphore()

    def greet(og, ob):
        pl.semaphore_signal(barrier, inc=1, device_id=(og, ob), device_id_type=MESH)

    each_peer(greet)

    loads[0].wait()
    numbers = jnp.broadcast_to(picks[...].astype(jnp.float32), (block, items)).T
    row = lax.broadcasted_iota(jnp.int32, (items, block), 0) % count
    lane = lax.broadcasted_iota(jnp.int32, (items, block), 1)
    base = (row // per_tile) * block
    hot = (numbers == (lane + base).astype(jnp.float32)).astype(jnp.float32)
    loads[1].wait()
    values = grads[...].astype(jnp.float32)
    packed = jnp.concatenate(
        [values.reshape(peers, count, block), hot.reshape(peers, count, block)], axis=1
    ).astype(jnp.bfloat16)
    send[...] = packed

    pl.semaphore_wait(barrier, peers - 1)

    def ship(og, ob):
        pltpu.make_async_remote_copy(
            src_ref=send.at[og * columns + ob],
            dst_ref=recv.at[me],
            send_sem=send_sem,
            recv_sem=recv_sem,
            device_id=(og, ob),
            device_id_type=MESH,
        ).start()

    each_peer(ship)
    for load in loads[3:]:
        load.start()
    recv[me] = send[me]

    loads[2].wait()
    table = slots[...].astype(jnp.float32)
    high = jnp.floor(table * (1.0 / 256.0))
    low = table - 256.0 * high
    rows = [part[:, t * block : (t + 1) * block] for part in (low, high) for t in range(tiles)]
    rows += [jnp.zeros((1, block), jnp.float32)] * (-len(rows) % 16)
    lookup[...] = jnp.concatenate(rows, axis=0).astype(jnp.bfloat16)

    for load in loads[3:]:
        load.wait()
    done = pltpu.make_async_remote_copy(
        src_ref=send.at[pl.ds(0, peers - 1)],
        dst_ref=recv.at[pl.ds(0, peers - 1)],
        send_sem=send_sem,
        recv_sem=recv_sem,
        device_id=place(0, 1),
        device_id_type=MESH,
    )
    done.wait_recv()
    done.wait_send()


def finish(recv, lookup, momentum, params, new_momentum_hbm, new_params_hbm,
           new_momentum, new_params, total, store_sem):
    peers, twice, block = recv.shape
    count = twice // 2
    owned = momentum.shape[0]
    width = owned // count
    per_tile = block // width
    tiles = owned // block
    group = min(peers, 256 // count)
    chunk = group * count
    cut = 128

    def fetch(i):
        got = recv[pl.ds(i * group, group)].astype(jnp.float32)
        vals = got[:, :count].reshape(chunk, block).astype(jnp.bfloat16)
        ones = got[:, count:].reshape(chunk, block).astype(jnp.bfloat16)
        found = lax.dot_general(
            lookup[...], ones, (((1,), (1,)), ((), ())), preferred_element_type=jnp.float32
        )
        where = lax.broadcasted_iota(jnp.int32, (1, chunk), 1) % count // per_tile
        slot = jnp.zeros((1, chunk), jnp.float32)
        for t in range(tiles):
            slot = jnp.where(
                where == t, found[t : t + 1] + 256.0 * found[tiles + t : tiles + t + 1], slot
            )
        return vals, slot.astype(jnp.int32)

    def add_up(vals, slot, first):
        number = lax.broadcasted_iota(jnp.int32, (cut, chunk), 0) + first
        put = (number == slot).astype(jnp.float32).astype(jnp.bfloat16)
        return jnp.dot(put, vals, preferred_element_type=jnp.float32)

    single = peers == group
    if single:
        vals, slot = fetch(0)
    else:
        total[...] = jnp.zeros_like(total)

        def step(i, c):
            v, s = fetch(i)
            for first in range(0, owned, cut):
                total[pl.ds(first, cut)] += add_up(v, s, first)
            return c

        lax.fori_loop(0, peers // group, step, 0)

    stores = []
    for n, first in enumerate(range(0, owned, cut)):
        at = pl.ds(first, cut)
        gradient = add_up(vals, slot, first) if single else total[at]
        moved = 0.9 * momentum[at] + gradient
        new_momentum[at] = moved
        new_params[at] = params[at] - 0.05 * (gradient + 0.9 * moved)
        for i, (source, target) in enumerate(
            [(new_momentum, new_momentum_hbm), (new_params, new_params_hbm)]
        ):
            store = pltpu.make_async_copy(source.at[at], target.at[at], store_sem.at[2 * n + i])
            store.start()
            stores.append(store)
    for store in stores:
        store.wait()


def shards(grads, picks, slot_map, momentum, params):
    groups = lax.axis_size("grp")
    columns = lax.axis_size("blk")
    peers = groups * columns
    items, block = grads.shape[1:]
    owned = slot_map.shape[1]
    count = items // peers
    vmem = pl.BlockSpec(memory_space=pltpu.VMEM)
    hbm = pl.BlockSpec(memory_space=pltpu.HBM)
    kept = jax.ShapeDtypeStruct((owned, block), jnp.float32)
    limit = 40 * 1024 * 1024
    arrived = pl.pallas_call(
        functools.partial(exchange, groups, columns),
        out_shape=(
            jax.ShapeDtypeStruct((peers, 2 * count, block), jnp.bfloat16),
            jax.ShapeDtypeStruct((16, block), jnp.bfloat16),
            kept,
            kept,
        ),
        in_specs=[hbm] * 5,
        out_specs=(vmem,) * 4,
        scratch_shapes=[
            pltpu.VMEM((items, block), jnp.bfloat16),
            pltpu.VMEM((1, items), jnp.int32),
            pltpu.VMEM((1, owned), jnp.int32),
            pltpu.VMEM((peers, 2 * count, block), jnp.bfloat16),
            pltpu.SemaphoreType.DMA((5,)),
            pltpu.SemaphoreType.DMA,
            pltpu.SemaphoreType.DMA,
        ],
        compiler_params=pltpu.CompilerParams(
            collective_id=0, has_side_effects=True, vmem_limit_bytes=limit
        ),
    )(*[
        pltpu.with_memory_space_constraint(x, pltpu.HBM)
        for x in (grads[0], picks, slot_map, momentum, params)
    ])
    return pl.pallas_call(
        finish,
        out_shape=(kept, kept),
        in_specs=[vmem] * 4,
        out_specs=(hbm, hbm),
        scratch_shapes=[
            pltpu.VMEM((owned, block), jnp.float32),
            pltpu.VMEM((owned, block), jnp.float32),
            pltpu.VMEM((owned, block), jnp.float32),
            pltpu.SemaphoreType.DMA((2 * owned // 128,)),
        ],
        compiler_params=pltpu.CompilerParams(vmem_limit_bytes=limit),
    )(*arrived)


def solution(mesh):
    placed = (
        P(("grp", "blk"), None, None),
        P(("grp", "blk"), None),
        P(("grp", "blk"), None),
        P(("grp", "blk"), None),
        P(("grp", "blk"), None),
    )
    return jax.shard_map(
        shards,
        mesh=mesh,
        in_specs=placed,
        out_specs=(P(("grp", "blk"), None), P(("grp", "blk"), None)),
        check_vma=False,
    )
```

```python
import functools

import jax
import jax.numpy as jnp
from jax import lax
from jax.experimental import pallas as pl
from jax.experimental.pallas import tpu as pltpu
from jax.sharding import PartitionSpec as P

MESH = pl.DeviceIdType.MESH


def powers(*sizes):
    return all(size & (size - 1) == 0 for size in sizes)


def exchange(groups, columns, grads_hbm, picks_hbm, slots_hbm, momentum_hbm, params_hbm,
             recv, lookup, momentum, params, grads, picks, slots, send,
             load_sem, send_sem, recv_sem):
    peers = groups * columns
    items, block = grads.shape
    owned = slots.shape[1]
    count = items // peers
    width = owned // count
    g = lax.axis_index("grp")
    b = lax.axis_index("blk")
    me = g * columns + b

    loads = [
        pltpu.make_async_copy(source, target, load_sem.at[i])
        for i, (source, target) in enumerate(
            [
                (picks_hbm, picks),
                (grads_hbm, grads),
                (slots_hbm, slots),
                (momentum_hbm, momentum),
                (params_hbm, params),
            ]
        )
    ]
    for load in loads[:3]:
        load.start()

    def place(dg, db):
        if powers(groups, columns):
            return g ^ dg, b ^ db
        return lax.rem(g + dg, groups), lax.rem(b + db, columns)

    def each_peer(act):
        if peers <= 64:
            for db in reversed(range(columns)):
                for dg in reversed(range(groups)):
                    if dg or db:
                        act(*place(dg, db))
        else:
            def step(k, c):
                act(*place(k // columns, lax.rem(k, columns)))
                return c

            lax.fori_loop(1, peers, step, 0)

    barrier = pltpu.get_barrier_semaphore()

    def greet(og, ob):
        pl.semaphore_signal(barrier, inc=1, device_id=(og, ob), device_id_type=MESH)

    each_peer(greet)

    loads[0].wait()
    halves = block // width
    rows = count // halves
    numbers = jnp.broadcast_to(picks[...].astype(jnp.float32), (block, items)).T
    numbers = numbers.reshape(peers, halves, rows, block)
    lane = lax.broadcasted_iota(jnp.int32, (peers, rows, block), 2)
    row = lax.broadcasted_iota(jnp.int32, (peers, rows, block), 1)
    half = lane // width
    target = (lane % width + (row + rows * half) * width).astype(jnp.float32)
    number = numbers[:, 0]
    for h in range(1, halves):
        number = jnp.where(half == h, numbers[:, h], number)
    send[:, halves] = (number == target).astype(jnp.float32).astype(jnp.bfloat16)
    loads[1].wait()
    values = grads[...].astype(jnp.float32).reshape(peers, halves, rows, block)
    send[:, :halves] = values.astype(jnp.bfloat16)

    pl.semaphore_wait(barrier, peers - 1)

    def ship(og, ob):
        pltpu.make_async_remote_copy(
            src_ref=send.at[og * columns + ob],
            dst_ref=recv.at[me],
            send_sem=send_sem,
            recv_sem=recv_sem,
            device_id=(og, ob),
            device_id_type=MESH,
        ).start()

    each_peer(ship)
    for load in loads[3:]:
        load.start()
    recv[me] = send[me]

    loads[2].wait()
    table = slots[...].astype(jnp.float32)
    high = jnp.floor(table * (1.0 / 256.0))
    low = table - 256.0 * high
    blank = jnp.zeros((1, width), jnp.float32)
    entries = []
    for part in (low, high):
        for j in range(count):
            mine = part[:, j * width : (j + 1) * width]
            entries.append(
                jnp.concatenate([mine if h == j // rows else blank for h in range(halves)], axis=1)
            )
    lookup[...] = jnp.concatenate(entries, axis=0).astype(jnp.bfloat16)

    for load in loads[3:]:
        load.wait()
    done = pltpu.make_async_remote_copy(
        src_ref=send.at[pl.ds(0, peers - 1)],
        dst_ref=recv.at[pl.ds(0, peers - 1)],
        send_sem=send_sem,
        recv_sem=recv_sem,
        device_id=place(0, 1),
        device_id_type=MESH,
    )
    done.wait_recv()
    done.wait_send()


def finish(recv, lookup, momentum, params, new_momentum_hbm, new_params_hbm,
           new_momentum, new_params, total, store_sem):
    peers, parts, rows, block = recv.shape
    halves = parts - 1
    count = halves * rows
    owned = momentum.shape[0]
    group = min(peers, 256 // count)
    chunk = group * count
    cut = 128

    def fetch(i):
        got = recv[pl.ds(i * group, group)].astype(jnp.float32)
        flat = [got[:, h].reshape(group * rows, block) for h in range(parts)]
        vals = jnp.concatenate(flat[:halves], axis=0).astype(jnp.bfloat16)
        found = lax.dot_general(
            lookup[...], flat[halves].astype(jnp.bfloat16), (((1,), (1,)), ((), ())),
            preferred_element_type=jnp.float32,
        )
        found = found[:count] + 256.0 * found[count:]
        where = lax.broadcasted_iota(jnp.int32, (1, group * rows), 1) % rows
        slots = []
        for h in range(halves):
            slot = found[h * rows : h * rows + 1]
            for r in range(1, rows):
                slot = jnp.where(where == r, found[h * rows + r : h * rows + r + 1], slot)
            slots.append(slot)
        return vals, jnp.concatenate(slots, axis=1).astype(jnp.int32)

    def add_up(vals, slot, first):
        number = lax.broadcasted_iota(jnp.int32, (cut, chunk), 0) + first
        put = (number == slot).astype(jnp.float32).astype(jnp.bfloat16)
        return jnp.dot(put, vals, preferred_element_type=jnp.float32)

    single = peers == group
    if single:
        vals, slot = fetch(0)
    else:
        total[...] = jnp.zeros_like(total)

        def step(i, c):
            v, s = fetch(i)
            for first in range(0, owned, cut):
                total[pl.ds(first, cut)] += add_up(v, s, first)
            return c

        lax.fori_loop(0, peers // group, step, 0)

    stores = []
    for n, first in enumerate(range(0, owned, cut)):
        at = pl.ds(first, cut)
        gradient = add_up(vals, slot, first) if single else total[at]
        moved = 0.9 * momentum[at] + gradient
        new_momentum[at] = moved
        new_params[at] = params[at] - 0.05 * (gradient + 0.9 * moved)
        for i, (source, target) in enumerate(
            [(new_momentum, new_momentum_hbm), (new_params, new_params_hbm)]
        ):
            store = pltpu.make_async_copy(source.at[at], target.at[at], store_sem.at[2 * n + i])
            store.start()
            stores.append(store)
    for store in stores:
        store.wait()


def shards(grads, picks, slot_map, momentum, params):
    groups = lax.axis_size("grp")
    columns = lax.axis_size("blk")
    peers = groups * columns
    items, block = grads.shape[1:]
    owned = slot_map.shape[1]
    count = items // peers
    halves = block * count // owned
    shape = (peers, halves + 1, count // halves, block)
    vmem = pl.BlockSpec(memory_space=pltpu.VMEM)
    hbm = pl.BlockSpec(memory_space=pltpu.HBM)
    kept = jax.ShapeDtypeStruct((owned, block), jnp.float32)
    limit = 40 * 1024 * 1024
    arrived = pl.pallas_call(
        functools.partial(exchange, groups, columns),
        out_shape=(
            jax.ShapeDtypeStruct(shape, jnp.bfloat16),
            jax.ShapeDtypeStruct((2 * count, block), jnp.bfloat16),
            kept,
            kept,
        ),
        in_specs=[hbm] * 5,
        out_specs=(vmem,) * 4,
        scratch_shapes=[
            pltpu.VMEM((items, block), jnp.bfloat16),
            pltpu.VMEM((1, items), jnp.int32),
            pltpu.VMEM((1, owned), jnp.int32),
            pltpu.VMEM(shape, jnp.bfloat16),
            pltpu.SemaphoreType.DMA((5,)),
            pltpu.SemaphoreType.DMA,
            pltpu.SemaphoreType.DMA,
        ],
        compiler_params=pltpu.CompilerParams(
            collective_id=0, has_side_effects=True, vmem_limit_bytes=limit
        ),
    )(*[
        pltpu.with_memory_space_constraint(x, pltpu.HBM)
        for x in (grads[0], picks, slot_map, momentum, params)
    ])
    return pl.pallas_call(
        finish,
        out_shape=(kept, kept),
        in_specs=[vmem] * 4,
        out_specs=(hbm, hbm),
        scratch_shapes=[
            pltpu.VMEM((owned, block), jnp.float32),
            pltpu.VMEM((owned, block), jnp.float32),
            pltpu.VMEM((owned, block), jnp.float32),
            pltpu.SemaphoreType.DMA((2 * owned // 128,)),
        ],
        compiler_params=pltpu.CompilerParams(vmem_limit_bytes=limit),
    )(*arrived)


def solution(mesh):
    placed = (
        P(("grp", "blk"), None, None),
        P(("grp", "blk"), None),
        P(("grp", "blk"), None),
        P(("grp", "blk"), None),
        P(("grp", "blk"), None),
    )
    return jax.shard_map(
        shards,
        mesh=mesh,
        in_specs=placed,
        out_specs=(P(("grp", "blk"), None), P(("grp", "blk"), None)),
        check_vma=False,
    )
```

```python
import functools

import jax
import jax.numpy as jnp
from jax import lax
from jax.experimental import pallas as pl
from jax.experimental.pallas import tpu as pltpu
from jax.sharding import PartitionSpec as P

LOGICAL = pl.DeviceIdType.LOGICAL


def powers(*sizes):
    return all(size & (size - 1) == 0 for size in sizes)


def exchange(groups, columns, grads_hbm, picks_hbm, slots_hbm, momentum_hbm, params_hbm,
             recv, lookup, momentum, params, grads, picks, slots, send,
             load_sem, send_sem, recv_sem):
    peers = groups * columns
    items, block = grads.shape
    owned = slots.shape[1]
    count = items // peers
    width = owned // count
    g = lax.axis_index("grp")
    b = lax.axis_index("blk")
    me = g * columns + b

    loads = [
        pltpu.make_async_copy(source, target, load_sem.at[i])
        for i, (source, target) in enumerate(
            [
                (picks_hbm, picks),
                (grads_hbm, grads),
                (slots_hbm, slots),
                (momentum_hbm, momentum),
                (params_hbm, params),
            ]
        )
    ]
    for load in loads[:3]:
        load.start()

    def place(k):
        return me ^ k if powers(peers) else lax.rem(me + k, peers)

    def each_peer(act):
        if peers <= 64:
            for db in reversed(range(columns)):
                for dg in reversed(range(groups)):
                    if dg or db:
                        act(place(dg * columns + db))
        else:
            def step(k, c):
                act(place(k))
                return c

            lax.fori_loop(1, peers, step, 0)

    barrier = pltpu.get_barrier_semaphore()

    def greet(other):
        pl.semaphore_signal(barrier, inc=1, device_id=other, device_id_type=LOGICAL)

    each_peer(greet)

    loads[0].wait()
    halves = block // width
    rows = count // halves
    numbers = jnp.broadcast_to(picks[...].astype(jnp.float32), (block, items)).T
    numbers = numbers.reshape(peers, halves, rows, block)
    lane = lax.broadcasted_iota(jnp.int32, (peers, rows, block), 2)
    row = lax.broadcasted_iota(jnp.int32, (peers, rows, block), 1)
    half = lane // width
    target = (lane % width + (row + rows * half) * width).astype(jnp.float32)
    number = numbers[:, 0]
    for h in range(1, halves):
        number = jnp.where(half == h, numbers[:, h], number)
    send[:, halves] = (number == target).astype(jnp.float32).astype(jnp.bfloat16)
    loads[1].wait()
    values = grads[...].astype(jnp.float32).reshape(peers, halves, rows, block)
    send[:, :halves] = values.astype(jnp.bfloat16)

    pl.semaphore_wait(barrier, peers - 1)

    def ship(other):
        pltpu.make_async_remote_copy(
            src_ref=send.at[other],
            dst_ref=recv.at[me],
            send_sem=send_sem,
            recv_sem=recv_sem,
            device_id=other,
            device_id_type=LOGICAL,
        ).start()

    each_peer(ship)
    for load in loads[3:]:
        load.start()
    recv[me] = send[me]

    loads[2].wait()
    table = slots[...].astype(jnp.float32)
    high = jnp.floor(table * (1.0 / 256.0))
    low = table - 256.0 * high
    blank = jnp.zeros((1, width), jnp.float32)
    entries = []
    for part in (low, high):
        for j in range(count):
            mine = part[:, j * width : (j + 1) * width]
            entries.append(
                jnp.concatenate([mine if h == j // rows else blank for h in range(halves)], axis=1)
            )
    lookup[...] = jnp.concatenate(entries, axis=0).astype(jnp.bfloat16)

    for load in loads[3:]:
        load.wait()
    done = pltpu.make_async_remote_copy(
        src_ref=send.at[pl.ds(0, peers - 1)],
        dst_ref=recv.at[pl.ds(0, peers - 1)],
        send_sem=send_sem,
        recv_sem=recv_sem,
        device_id=place(1),
        device_id_type=LOGICAL,
    )
    done.wait_recv()
    done.wait_send()


def finish(recv, lookup, momentum, params, new_momentum_hbm, new_params_hbm,
           new_momentum, new_params, total, store_sem):
    peers, parts, rows, block = recv.shape
    halves = parts - 1
    count = halves * rows
    owned = momentum.shape[0]
    group = min(peers, 256 // count)
    chunk = group * count
    cut = 128

    def fetch(i):
        got = recv[pl.ds(i * group, group)].astype(jnp.float32)
        flat = [got[:, h].reshape(group * rows, block) for h in range(parts)]
        vals = jnp.concatenate(flat[:halves], axis=0).astype(jnp.bfloat16)
        found = lax.dot_general(
            lookup[...], flat[halves].astype(jnp.bfloat16), (((1,), (1,)), ((), ())),
            preferred_element_type=jnp.float32,
        )
        found = found[:count] + 256.0 * found[count:]
        where = lax.broadcasted_iota(jnp.int32, (1, group * rows), 1) % rows
        slots = []
        for h in range(halves):
            slot = found[h * rows : h * rows + 1]
            for r in range(1, rows):
                slot = jnp.where(where == r, found[h * rows + r : h * rows + r + 1], slot)
            slots.append(slot)
        return vals, jnp.concatenate(slots, axis=1).astype(jnp.int32)

    def add_up(vals, slot, first):
        number = lax.broadcasted_iota(jnp.int32, (cut, chunk), 0) + first
        put = (number == slot).astype(jnp.float32).astype(jnp.bfloat16)
        return jnp.dot(put, vals, preferred_element_type=jnp.float32)

    single = peers == group
    if single:
        vals, slot = fetch(0)
    else:
        total[...] = jnp.zeros_like(total)

        def step(i, c):
            v, s = fetch(i)
            for first in range(0, owned, cut):
                total[pl.ds(first, cut)] += add_up(v, s, first)
            return c

        lax.fori_loop(0, peers // group, step, 0)

    stores = []
    for n, first in enumerate(range(0, owned, cut)):
        at = pl.ds(first, cut)
        gradient = add_up(vals, slot, first) if single else total[at]
        moved = 0.9 * momentum[at] + gradient
        new_momentum[at] = moved
        new_params[at] = params[at] - 0.05 * (gradient + 0.9 * moved)
        for i, (source, target) in enumerate(
            [(new_momentum, new_momentum_hbm), (new_params, new_params_hbm)]
        ):
            store = pltpu.make_async_copy(source.at[at], target.at[at], store_sem.at[2 * n + i])
            store.start()
            stores.append(store)
    for store in stores:
        store.wait()


def shards(grads, picks, slot_map, momentum, params):
    groups = lax.axis_size("grp")
    columns = lax.axis_size("blk")
    peers = groups * columns
    items, block = grads.shape[1:]
    owned = slot_map.shape[1]
    count = items // peers
    halves = block * count // owned
    shape = (peers, halves + 1, count // halves, block)
    vmem = pl.BlockSpec(memory_space=pltpu.VMEM)
    hbm = pl.BlockSpec(memory_space=pltpu.HBM)
    kept = jax.ShapeDtypeStruct((owned, block), jnp.float32)
    limit = 40 * 1024 * 1024
    arrived = pl.pallas_call(
        functools.partial(exchange, groups, columns),
        out_shape=(
            jax.ShapeDtypeStruct(shape, jnp.bfloat16),
            jax.ShapeDtypeStruct((2 * count, block), jnp.bfloat16),
            kept,
            kept,
        ),
        in_specs=[hbm] * 5,
        out_specs=(vmem,) * 4,
        scratch_shapes=[
            pltpu.VMEM((items, block), jnp.bfloat16),
            pltpu.VMEM((1, items), jnp.int32),
            pltpu.VMEM((1, owned), jnp.int32),
            pltpu.VMEM(shape, jnp.bfloat16),
            pltpu.SemaphoreType.DMA((5,)),
            pltpu.SemaphoreType.DMA,
            pltpu.SemaphoreType.DMA,
        ],
        compiler_params=pltpu.CompilerParams(
            collective_id=0, has_side_effects=True, vmem_limit_bytes=limit
        ),
    )(*[
        pltpu.with_memory_space_constraint(x, pltpu.HBM)
        for x in (grads[0], picks, slot_map, momentum, params)
    ])
    return pl.pallas_call(
        finish,
        out_shape=(kept, kept),
        in_specs=[vmem] * 4,
        out_specs=(hbm, hbm),
        scratch_shapes=[
            pltpu.VMEM((owned, block), jnp.float32),
            pltpu.VMEM((owned, block), jnp.float32),
            pltpu.VMEM((owned, block), jnp.float32),
            pltpu.SemaphoreType.DMA((2 * owned // 128,)),
        ],
        compiler_params=pltpu.CompilerParams(vmem_limit_bytes=limit),
    )(*arrived)


def solution(mesh):
    placed = (
        P(("grp", "blk"), None, None),
        P(("grp", "blk"), None),
        P(("grp", "blk"), None),
        P(("grp", "blk"), None),
        P(("grp", "blk"), None),
    )
    return jax.shard_map(
        shards,
        mesh=mesh,
        in_specs=placed,
        out_specs=(P(("grp", "blk"), None), P(("grp", "blk"), None)),
        check_vma=False,
    )
```

```python
import functools

import jax
import jax.numpy as jnp
from jax import lax
from jax.experimental import pallas as pl
from jax.experimental.pallas import tpu as pltpu
from jax.sharding import PartitionSpec as P

LOGICAL = pl.DeviceIdType.LOGICAL


def powers(*sizes):
    return all(size & (size - 1) == 0 for size in sizes)


def exchange(groups, columns, grads_hbm, picks_hbm, slots_hbm, momentum_hbm, params_hbm,
             recv, lookup, momentum, params, grads, picks, slots, send,
             load_sem, send_sem, recv_sem):
    peers = groups * columns
    items, block = grads.shape
    owned = slots.shape[1]
    count = items // peers
    width = owned // count
    g = lax.axis_index("grp")
    b = lax.axis_index("blk")
    me = g * columns + b

    loads = [
        pltpu.make_async_copy(source, target, load_sem.at[i])
        for i, (source, target) in enumerate(
            [
                (picks_hbm, picks),
                (grads_hbm, grads),
                (slots_hbm, slots),
                (momentum_hbm, momentum),
                (params_hbm, params),
            ]
        )
    ]
    for load in loads[:3]:
        load.start()

    def place(k):
        return me ^ k if powers(peers) else lax.rem(me + k, peers)

    def each_peer(act):
        if peers <= 64:
            for db in reversed(range(columns)):
                for dg in reversed(range(groups)):
                    if dg or db:
                        act(place(dg * columns + db))
        else:
            def step(k, c):
                act(place(k))
                return c

            lax.fori_loop(1, peers, step, 0)

    barrier = pltpu.get_barrier_semaphore()

    def greet(other):
        pl.semaphore_signal(barrier, inc=1, device_id=other, device_id_type=LOGICAL)

    each_peer(greet)
    for load in loads[3:]:
        load.start()

    loads[0].wait()
    halves = block // width
    rows = count // halves
    numbers = jnp.broadcast_to(picks[...].astype(jnp.float32), (block, items)).T
    numbers = numbers.reshape(peers, halves, rows, block)
    lane = lax.broadcasted_iota(jnp.int32, (peers, rows, block), 2)
    row = lax.broadcasted_iota(jnp.int32, (peers, rows, block), 1)
    half = lane // width
    target = (lane % width + (row + rows * half) * width).astype(jnp.float32)
    number = numbers[:, 0]
    for h in range(1, halves):
        number = jnp.where(half == h, numbers[:, h], number)
    send[:, halves] = (number == target).astype(jnp.float32).astype(jnp.bfloat16)
    loads[1].wait()
    values = grads[...].astype(jnp.float32).reshape(peers, halves, rows, block)
    send[:, :halves] = values.astype(jnp.bfloat16)

    pl.semaphore_wait(barrier, peers - 1)

    def ship(other):
        pltpu.make_async_remote_copy(
            src_ref=send.at[other],
            dst_ref=recv.at[me],
            send_sem=send_sem,
            recv_sem=recv_sem,
            device_id=other,
            device_id_type=LOGICAL,
        ).start()

    each_peer(ship)
    recv[me] = send[me]

    loads[2].wait()
    table = slots[...].astype(jnp.float32)
    high = jnp.floor(table * (1.0 / 256.0))
    low = table - 256.0 * high
    blank = jnp.zeros((1, width), jnp.float32)
    entries = []
    for part in (low, high):
        for j in range(count):
            mine = part[:, j * width : (j + 1) * width]
            entries.append(
                jnp.concatenate([mine if h == j // rows else blank for h in range(halves)], axis=1)
            )
    lookup[...] = jnp.concatenate(entries, axis=0).astype(jnp.bfloat16)

    for load in loads[3:]:
        load.wait()
    done = pltpu.make_async_remote_copy(
        src_ref=send.at[pl.ds(0, peers - 1)],
        dst_ref=recv.at[pl.ds(0, peers - 1)],
        send_sem=send_sem,
        recv_sem=recv_sem,
        device_id=place(1),
        device_id_type=LOGICAL,
    )
    done.wait_recv()
    done.wait_send()


def finish(recv, lookup, momentum, params, new_momentum_hbm, new_params_hbm,
           new_momentum, new_params, total, store_sem):
    peers, parts, rows, block = recv.shape
    halves = parts - 1
    count = halves * rows
    owned = momentum.shape[0]
    group = min(peers, 256 // count)
    chunk = group * count
    cut = 128

    def fetch(i):
        got = recv[pl.ds(i * group, group)].astype(jnp.float32)
        flat = [got[:, h].reshape(group * rows, block) for h in range(parts)]
        vals = jnp.concatenate(flat[:halves], axis=0).astype(jnp.bfloat16)
        found = lax.dot_general(
            lookup[...], flat[halves].astype(jnp.bfloat16), (((1,), (1,)), ((), ())),
            preferred_element_type=jnp.float32,
        )
        found = found[:count] + 256.0 * found[count:]
        where = lax.broadcasted_iota(jnp.int32, (1, group * rows), 1) % rows
        slots = []
        for h in range(halves):
            slot = found[h * rows : h * rows + 1]
            for r in range(1, rows):
                slot = jnp.where(where == r, found[h * rows + r : h * rows + r + 1], slot)
            slots.append(slot)
        return vals, jnp.concatenate(slots, axis=1).astype(jnp.int32)

    def add_up(vals, slot, first):
        number = lax.broadcasted_iota(jnp.int32, (cut, chunk), 0) + first
        put = (number == slot).astype(jnp.float32).astype(jnp.bfloat16)
        return jnp.dot(put, vals, preferred_element_type=jnp.float32)

    single = peers == group
    if single:
        vals, slot = fetch(0)
    else:
        total[...] = jnp.zeros_like(total)

        def step(i, c):
            v, s = fetch(i)
            for first in range(0, owned, cut):
                total[pl.ds(first, cut)] += add_up(v, s, first)
            return c

        lax.fori_loop(0, peers // group, step, 0)

    stores = []
    for n, first in enumerate(range(0, owned, cut)):
        at = pl.ds(first, cut)
        gradient = add_up(vals, slot, first) if single else total[at]
        moved = 0.9 * momentum[at] + gradient
        new_momentum[at] = moved
        new_params[at] = params[at] - 0.05 * (gradient + 0.9 * moved)
        for i, (source, target) in enumerate(
            [(new_momentum, new_momentum_hbm), (new_params, new_params_hbm)]
        ):
            store = pltpu.make_async_copy(source.at[at], target.at[at], store_sem.at[2 * n + i])
            store.start()
            stores.append(store)
    for store in stores:
        store.wait()


def shards(grads, picks, slot_map, momentum, params):
    groups = lax.axis_size("grp")
    columns = lax.axis_size("blk")
    peers = groups * columns
    items, block = grads.shape[1:]
    owned = slot_map.shape[1]
    count = items // peers
    halves = block * count // owned
    shape = (peers, halves + 1, count // halves, block)
    vmem = pl.BlockSpec(memory_space=pltpu.VMEM)
    hbm = pl.BlockSpec(memory_space=pltpu.HBM)
    kept = jax.ShapeDtypeStruct((owned, block), jnp.float32)
    limit = 40 * 1024 * 1024
    arrived = pl.pallas_call(
        functools.partial(exchange, groups, columns),
        out_shape=(
            jax.ShapeDtypeStruct(shape, jnp.bfloat16),
            jax.ShapeDtypeStruct((2 * count, block), jnp.bfloat16),
            kept,
            kept,
        ),
        in_specs=[hbm] * 5,
        out_specs=(vmem,) * 4,
        scratch_shapes=[
            pltpu.VMEM((items, block), jnp.bfloat16),
            pltpu.VMEM((1, items), jnp.int32),
            pltpu.VMEM((1, owned), jnp.int32),
            pltpu.VMEM(shape, jnp.bfloat16),
            pltpu.SemaphoreType.DMA((5,)),
            pltpu.SemaphoreType.DMA,
            pltpu.SemaphoreType.DMA,
        ],
        compiler_params=pltpu.CompilerParams(
            collective_id=0, has_side_effects=True, vmem_limit_bytes=limit
        ),
    )(*[
        pltpu.with_memory_space_constraint(x, pltpu.HBM)
        for x in (grads[0], picks, slot_map, momentum, params)
    ])
    return pl.pallas_call(
        finish,
        out_shape=(kept, kept),
        in_specs=[vmem] * 4,
        out_specs=(hbm, hbm),
        scratch_shapes=[
            pltpu.VMEM((owned, block), jnp.float32),
            pltpu.VMEM((owned, block), jnp.float32),
            pltpu.VMEM((owned, block), jnp.float32),
            pltpu.SemaphoreType.DMA((2 * owned // 128,)),
        ],
        compiler_params=pltpu.CompilerParams(vmem_limit_bytes=limit),
    )(*arrived)


def solution(mesh):
    placed = (
        P(("grp", "blk"), None, None),
        P(("grp", "blk"), None),
        P(("grp", "blk"), None),
        P(("grp", "blk"), None),
        P(("grp", "blk"), None),
    )
    return jax.shard_map(
        shards,
        mesh=mesh,
        in_specs=placed,
        out_specs=(P(("grp", "blk"), None), P(("grp", "blk"), None)),
        check_vma=False,
    )
```

```python
import functools

import jax
import jax.numpy as jnp
from jax import lax
from jax.experimental import pallas as pl
from jax.experimental.pallas import tpu as pltpu
from jax.sharding import PartitionSpec as P

LOGICAL = pl.DeviceIdType.LOGICAL


def powers(*sizes):
    return all(size & (size - 1) == 0 for size in sizes)


def exchange(groups, columns, grads_hbm, picks_hbm, slots_hbm, momentum_hbm, params_hbm,
             recv, lookup, momentum, params, grads, picks, slots, send,
             load_sem, send_sem, recv_sem):
    peers = groups * columns
    items, block = grads.shape
    owned = slots.shape[1]
    count = items // peers
    width = owned // count
    g = lax.axis_index("grp")
    b = lax.axis_index("blk")
    me = g * columns + b

    loads = [
        pltpu.make_async_copy(source, target, load_sem.at[i])
        for i, (source, target) in enumerate(
            [
                (picks_hbm, picks),
                (grads_hbm, grads),
                (slots_hbm, slots),
                (momentum_hbm, momentum),
                (params_hbm, params),
            ]
        )
    ]
    for load in loads[:3]:
        load.start()

    def place(k):
        return me ^ k if powers(peers) else lax.rem(me + k, peers)

    def each_peer(act):
        if peers <= 64:
            for db in reversed(range(columns)):
                for dg in reversed(range(groups)):
                    if dg or db:
                        act(place(dg * columns + db))
        else:
            def step(k, c):
                act(place(k))
                return c

            lax.fori_loop(1, peers, step, 0)

    barrier = pltpu.get_barrier_semaphore()

    def greet(other):
        pl.semaphore_signal(barrier, inc=1, device_id=other, device_id_type=LOGICAL)

    each_peer(greet)

    loads[0].wait()
    halves = block // width
    rows = count // halves
    numbers = jnp.broadcast_to(picks[...].astype(jnp.float32), (block, items)).T
    numbers = numbers.reshape(peers, halves, rows, block)
    lane = lax.broadcasted_iota(jnp.int32, (peers, rows, block), 2)
    row = lax.broadcasted_iota(jnp.int32, (peers, rows, block), 1)
    half = lane // width
    target = (lane % width + (row + rows * half) * width).astype(jnp.float32)
    number = numbers[:, 0]
    for h in range(1, halves):
        number = jnp.where(half == h, numbers[:, h], number)
    send[:, halves] = (number == target).astype(jnp.float32).astype(jnp.bfloat16)
    loads[1].wait()
    values = grads[...].astype(jnp.float32).reshape(peers, halves, rows, block)
    send[:, :halves] = values.astype(jnp.bfloat16)

    pl.semaphore_wait(barrier, peers - 1)

    def ship(other):
        pltpu.make_async_remote_copy(
            src_ref=send.at[other],
            dst_ref=recv.at[me],
            send_sem=send_sem,
            recv_sem=recv_sem,
            device_id=other,
            device_id_type=LOGICAL,
        ).start()

    each_peer(ship)
    for load in loads[3:]:
        load.start()
    recv[me] = send[me]

    loads[2].wait()
    table = slots[...].astype(jnp.float32)
    high = jnp.floor(table * (1.0 / 256.0))
    low = table - 256.0 * high
    blank = jnp.zeros((1, width), jnp.float32)
    entries = []
    for part in (low, high):
        for j in range(count):
            mine = part[:, j * width : (j + 1) * width]
            entries.append(
                jnp.concatenate([mine if h == j // rows else blank for h in range(halves)], axis=1)
            )
    lookup[...] = jnp.concatenate(entries, axis=0).astype(jnp.bfloat16)

    for load in loads[3:]:
        load.wait()
    done = pltpu.make_async_remote_copy(
        src_ref=send.at[pl.ds(0, peers - 1)],
        dst_ref=recv.at[pl.ds(0, peers - 1)],
        send_sem=send_sem,
        recv_sem=recv_sem,
        device_id=place(1),
        device_id_type=LOGICAL,
    )
    done.wait_recv()
    done.wait_send()


def finish(recv, lookup, momentum, params, new_momentum_hbm, new_params_hbm,
           new_momentum, new_params, total, store_sem):
    peers, parts, rows, block = recv.shape
    halves = parts - 1
    count = halves * rows
    owned = momentum.shape[0]
    group = min(peers, 256 // count)
    chunk = group * count
    cut = 256

    def fetch(i):
        got = recv[pl.ds(i * group, group)].astype(jnp.float32)
        flat = [got[:, h].reshape(group * rows, block) for h in range(parts)]
        vals = jnp.concatenate(flat[:halves], axis=0).astype(jnp.bfloat16)
        found = lax.dot_general(
            lookup[...], flat[halves].astype(jnp.bfloat16), (((1,), (1,)), ((), ())),
            preferred_element_type=jnp.float32,
        )
        found = found[:count] + 256.0 * found[count:]
        where = lax.broadcasted_iota(jnp.int32, (1, group * rows), 1) % rows
        slots = []
        for h in range(halves):
            slot = found[h * rows : h * rows + 1]
            for r in range(1, rows):
                slot = jnp.where(where == r, found[h * rows + r : h * rows + r + 1], slot)
            slots.append(slot)
        return vals, jnp.concatenate(slots, axis=1).astype(jnp.int32)

    def add_up(vals, slot, first):
        number = lax.broadcasted_iota(jnp.int32, (cut, chunk), 0) + first
        put = (number == slot).astype(jnp.float32).astype(jnp.bfloat16)
        return jnp.dot(put, vals, preferred_element_type=jnp.float32)

    single = peers == group
    if single:
        vals, slot = fetch(0)
    else:
        total[...] = jnp.zeros_like(total)

        def step(i, c):
            v, s = fetch(i)
            for first in range(0, owned, cut):
                total[pl.ds(first, cut)] += add_up(v, s, first)
            return c

        lax.fori_loop(0, peers // group, step, 0)

    stores = []
    for n, first in enumerate(range(0, owned, cut)):
        at = pl.ds(first, cut)
        gradient = add_up(vals, slot, first) if single else total[at]
        moved = 0.9 * momentum[at] + gradient
        new_momentum[at] = moved
        new_params[at] = params[at] - 0.05 * (gradient + 0.9 * moved)
        for i, (source, target) in enumerate(
            [(new_momentum, new_momentum_hbm), (new_params, new_params_hbm)]
        ):
            store = pltpu.make_async_copy(source.at[at], target.at[at], store_sem.at[2 * n + i])
            store.start()
            stores.append(store)
    for store in stores:
        store.wait()


def shards(grads, picks, slot_map, momentum, params):
    groups = lax.axis_size("grp")
    columns = lax.axis_size("blk")
    peers = groups * columns
    items, block = grads.shape[1:]
    owned = slot_map.shape[1]
    count = items // peers
    halves = block * count // owned
    shape = (peers, halves + 1, count // halves, block)
    vmem = pl.BlockSpec(memory_space=pltpu.VMEM)
    hbm = pl.BlockSpec(memory_space=pltpu.HBM)
    kept = jax.ShapeDtypeStruct((owned, block), jnp.float32)
    limit = 40 * 1024 * 1024
    arrived = pl.pallas_call(
        functools.partial(exchange, groups, columns),
        out_shape=(
            jax.ShapeDtypeStruct(shape, jnp.bfloat16),
            jax.ShapeDtypeStruct((2 * count, block), jnp.bfloat16),
            kept,
            kept,
        ),
        in_specs=[hbm] * 5,
        out_specs=(vmem,) * 4,
        scratch_shapes=[
            pltpu.VMEM((items, block), jnp.bfloat16),
            pltpu.VMEM((1, items), jnp.int32),
            pltpu.VMEM((1, owned), jnp.int32),
            pltpu.VMEM(shape, jnp.bfloat16),
            pltpu.SemaphoreType.DMA((5,)),
            pltpu.SemaphoreType.DMA,
            pltpu.SemaphoreType.DMA,
        ],
        compiler_params=pltpu.CompilerParams(
            collective_id=0, has_side_effects=True, vmem_limit_bytes=limit
        ),
    )(*[
        pltpu.with_memory_space_constraint(x, pltpu.HBM)
        for x in (grads[0], picks, slot_map, momentum, params)
    ])
    return pl.pallas_call(
        finish,
        out_shape=(kept, kept),
        in_specs=[vmem] * 4,
        out_specs=(hbm, hbm),
        scratch_shapes=[
            pltpu.VMEM((owned, block), jnp.float32),
            pltpu.VMEM((owned, block), jnp.float32),
            pltpu.VMEM((owned, block), jnp.float32),
            pltpu.SemaphoreType.DMA((2 * owned // 256,)),
        ],
        compiler_params=pltpu.CompilerParams(vmem_limit_bytes=limit),
    )(*arrived)


def solution(mesh):
    placed = (
        P(("grp", "blk"), None, None),
        P(("grp", "blk"), None),
        P(("grp", "blk"), None),
        P(("grp", "blk"), None),
        P(("grp", "blk"), None),
    )
    return jax.shard_map(
        shards,
        mesh=mesh,
        in_specs=placed,
        out_specs=(P(("grp", "blk"), None), P(("grp", "blk"), None)),
        check_vma=False,
    )
```

```python
import functools

import jax
import jax.numpy as jnp
from jax import lax
from jax.experimental import pallas as pl
from jax.experimental.pallas import tpu as pltpu
from jax.sharding import PartitionSpec as P

LOGICAL = pl.DeviceIdType.LOGICAL


def powers(*sizes):
    return all(size & (size - 1) == 0 for size in sizes)


def exchange(groups, columns, grads_hbm, picks_hbm, slots_hbm, momentum_hbm, params_hbm,
             recv, lookup, momentum, params, grads, picks, slots, send,
             load_sem, send_sem, recv_sem):
    peers = groups * columns
    items, block = grads.shape
    owned = slots.shape[1]
    count = items // peers
    width = owned // count
    g = lax.axis_index("grp")
    b = lax.axis_index("blk")
    me = g * columns + b

    loads = [
        pltpu.make_async_copy(source, target, load_sem.at[i])
        for i, (source, target) in enumerate(
            [
                (picks_hbm, picks),
                (grads_hbm, grads),
                (slots_hbm, slots),
                (momentum_hbm, momentum),
                (params_hbm, params),
            ]
        )
    ]
    for load in loads[:3]:
        load.start()

    def place(k):
        return me ^ k if powers(peers) else lax.rem(me + k, peers)

    def each_peer(act):
        if peers <= 64:
            for dg in reversed(range(groups)):
                for db in reversed(range(columns)):
                    if dg or db:
                        act(place(dg * columns + db))
        else:
            def step(k, c):
                act(place(k))
                return c

            lax.fori_loop(1, peers, step, 0)

    barrier = pltpu.get_barrier_semaphore()

    def greet(other):
        pl.semaphore_signal(barrier, inc=1, device_id=other, device_id_type=LOGICAL)

    each_peer(greet)

    loads[0].wait()
    halves = block // width
    rows = count // halves
    numbers = jnp.broadcast_to(picks[...].astype(jnp.float32), (block, items)).T
    numbers = numbers.reshape(peers, halves, rows, block)
    lane = lax.broadcasted_iota(jnp.int32, (peers, rows, block), 2)
    row = lax.broadcasted_iota(jnp.int32, (peers, rows, block), 1)
    half = lane // width
    target = (lane % width + (row + rows * half) * width).astype(jnp.float32)
    number = numbers[:, 0]
    for h in range(1, halves):
        number = jnp.where(half == h, numbers[:, h], number)
    send[:, halves] = (number == target).astype(jnp.float32).astype(jnp.bfloat16)
    loads[1].wait()
    values = grads[...].astype(jnp.float32).reshape(peers, halves, rows, block)
    send[:, :halves] = values.astype(jnp.bfloat16)

    pl.semaphore_wait(barrier, peers - 1)

    def ship(other):
        pltpu.make_async_remote_copy(
            src_ref=send.at[other],
            dst_ref=recv.at[me],
            send_sem=send_sem,
            recv_sem=recv_sem,
            device_id=other,
            device_id_type=LOGICAL,
        ).start()

    each_peer(ship)
    for load in loads[3:]:
        load.start()
    recv[me] = send[me]

    loads[2].wait()
    table = slots[...].astype(jnp.float32)
    high = jnp.floor(table * (1.0 / 256.0))
    low = table - 256.0 * high
    blank = jnp.zeros((1, width), jnp.float32)
    entries = []
    for part in (low, high):
        for j in range(count):
            mine = part[:, j * width : (j + 1) * width]
            entries.append(
                jnp.concatenate([mine if h == j // rows else blank for h in range(halves)], axis=1)
            )
    lookup[...] = jnp.concatenate(entries, axis=0).astype(jnp.bfloat16)

    for load in loads[3:]:
        load.wait()
    done = pltpu.make_async_remote_copy(
        src_ref=send.at[pl.ds(0, peers - 1)],
        dst_ref=recv.at[pl.ds(0, peers - 1)],
        send_sem=send_sem,
        recv_sem=recv_sem,
        device_id=place(1),
        device_id_type=LOGICAL,
    )
    done.wait_recv()
    done.wait_send()


def finish(recv, lookup, momentum, params, new_momentum_hbm, new_params_hbm,
           new_momentum, new_params, total, store_sem):
    peers, parts, rows, block = recv.shape
    halves = parts - 1
    count = halves * rows
    owned = momentum.shape[0]
    group = min(peers, 256 // count)
    chunk = group * count
    cut = 256

    def fetch(i):
        got = recv[pl.ds(i * group, group)].astype(jnp.float32)
        flat = [got[:, h].reshape(group * rows, block) for h in range(parts)]
        vals = jnp.concatenate(flat[:halves], axis=0).astype(jnp.bfloat16)
        found = lax.dot_general(
            lookup[...], flat[halves].astype(jnp.bfloat16), (((1,), (1,)), ((), ())),
            preferred_element_type=jnp.float32,
        )
        found = found[:count] + 256.0 * found[count:]
        where = lax.broadcasted_iota(jnp.int32, (1, group * rows), 1) % rows
        slots = []
        for h in range(halves):
            slot = found[h * rows : h * rows + 1]
            for r in range(1, rows):
                slot = jnp.where(where == r, found[h * rows + r : h * rows + r + 1], slot)
            slots.append(slot)
        return vals, jnp.concatenate(slots, axis=1).astype(jnp.int32)

    def add_up(vals, slot, first):
        number = lax.broadcasted_iota(jnp.int32, (cut, chunk), 0) + first
        put = (number == slot).astype(jnp.float32).astype(jnp.bfloat16)
        return jnp.dot(put, vals, preferred_element_type=jnp.float32)

    single = peers == group
    if single:
        vals, slot = fetch(0)
    else:
        total[...] = jnp.zeros_like(total)

        def step(i, c):
            v, s = fetch(i)
            for first in range(0, owned, cut):
                total[pl.ds(first, cut)] += add_up(v, s, first)
            return c

        lax.fori_loop(0, peers // group, step, 0)

    stores = []
    for n, first in enumerate(range(0, owned, cut)):
        at = pl.ds(first, cut)
        gradient = add_up(vals, slot, first) if single else total[at]
        moved = 0.9 * momentum[at] + gradient
        new_momentum[at] = moved
        new_params[at] = params[at] - 0.05 * (gradient + 0.9 * moved)
        for i, (source, target) in enumerate(
            [(new_momentum, new_momentum_hbm), (new_params, new_params_hbm)]
        ):
            store = pltpu.make_async_copy(source.at[at], target.at[at], store_sem.at[2 * n + i])
            store.start()
            stores.append(store)
    for store in stores:
        store.wait()


def shards(grads, picks, slot_map, momentum, params):
    groups = lax.axis_size("grp")
    columns = lax.axis_size("blk")
    peers = groups * columns
    items, block = grads.shape[1:]
    owned = slot_map.shape[1]
    count = items // peers
    halves = block * count // owned
    shape = (peers, halves + 1, count // halves, block)
    vmem = pl.BlockSpec(memory_space=pltpu.VMEM)
    hbm = pl.BlockSpec(memory_space=pltpu.HBM)
    kept = jax.ShapeDtypeStruct((owned, block), jnp.float32)
    limit = 40 * 1024 * 1024
    arrived = pl.pallas_call(
        functools.partial(exchange, groups, columns),
        out_shape=(
            jax.ShapeDtypeStruct(shape, jnp.bfloat16),
            jax.ShapeDtypeStruct((2 * count, block), jnp.bfloat16),
            kept,
            kept,
        ),
        in_specs=[hbm] * 5,
        out_specs=(vmem,) * 4,
        scratch_shapes=[
            pltpu.VMEM((items, block), jnp.bfloat16),
            pltpu.VMEM((1, items), jnp.int32),
            pltpu.VMEM((1, owned), jnp.int32),
            pltpu.VMEM(shape, jnp.bfloat16),
            pltpu.SemaphoreType.DMA((5,)),
            pltpu.SemaphoreType.DMA,
            pltpu.SemaphoreType.DMA,
        ],
        compiler_params=pltpu.CompilerParams(
            collective_id=0, has_side_effects=True, vmem_limit_bytes=limit
        ),
    )(*[
        pltpu.with_memory_space_constraint(x, pltpu.HBM)
        for x in (grads[0], picks, slot_map, momentum, params)
    ])
    return pl.pallas_call(
        finish,
        out_shape=(kept, kept),
        in_specs=[vmem] * 4,
        out_specs=(hbm, hbm),
        scratch_shapes=[
            pltpu.VMEM((owned, block), jnp.float32),
            pltpu.VMEM((owned, block), jnp.float32),
            pltpu.VMEM((owned, block), jnp.float32),
            pltpu.SemaphoreType.DMA((2 * owned // 256,)),
        ],
        compiler_params=pltpu.CompilerParams(vmem_limit_bytes=limit),
    )(*arrived)


def solution(mesh):
    placed = (
        P(("grp", "blk"), None, None),
        P(("grp", "blk"), None),
        P(("grp", "blk"), None),
        P(("grp", "blk"), None),
        P(("grp", "blk"), None),
    )
    return jax.shard_map(
        shards,
        mesh=mesh,
        in_specs=placed,
        out_specs=(P(("grp", "blk"), None), P(("grp", "blk"), None)),
        check_vma=False,
    )
```
